32 devices in a mesh: rep: 2 (over x), exp: 16 (over z, y, core).
Axes of the slice: x: 2, y: 2, z: 4, core: 2. Of those that a mesh axis runs over, the one named last changes fastest.
Arguments:
- tokens: bfloat16 [384, 2048], P('exp', 'rep'), may hold values from -6 to 6
- cotangent: bfloat16 [384, 2048], P('exp', 'rep'), may hold values from -6 to 6
- router_weight: bfloat16 [384, 4], P('exp'), may hold values from 0.019897461 to 0.5
- expert_ids: int32 [384, 4], P('exp'), may hold values from 0 to 15, all different within a row; in each aligned block of 24 rows (0 to 23, 24 to 47, ...) at most 9 rows name the same one
- w_gate: bfloat16 [16, 2048, 768], P('exp', 'rep'), may hold values from -0.125 to 0.125
- w_up: bfloat16 [16, 2048, 768], P('exp', 'rep'), may hold values from -0.125 to 0.125
- w_down: bfloat16 [16, 768, 2048], P('exp', None, 'rep'), may hold values from -0.21875 to 0.21875
Outputs:
- mixed: bfloat16 [384, 2048], P('exp', 'rep')
- token_grad: bfloat16 [384, 2048], P('exp', 'rep')
- router_grad: bfloat16 [384, 4], P('exp')
- gate_weight_grad: bfloat16 [16, 2048, 768], P('exp', 'rep')
- up_weight_grad: bfloat16 [16, 2048, 768], P('exp', 'rep')
- down_weight_grad: bfloat16 [16, 768, 2048], P('exp', None, 'rep')
The draws below stay inside these ranges and needn't reach their ends.
Inputs may be any that keep to these rules, and one draw needn't show every extreme that they name: `expert_ids`: each row names 4 different experts. Among the 24 rows of one index of exp (aligned blocks) no expert is named more than 9 times, a bound that some block reaches.
All inputs are finite; a program needn't handle non-finite values.
Results may differ from the reference program's by a relative error of at most 0.013.
Values may be sent and summed in bfloat16 or wider, within the bound.
A program may use at most 64 MiB of HBM per device.

```python
import math
import jax
import jax.numpy as jnp
import numpy as np
from jax import lax

D = 2048
FF = 768
TOK_DEV = 24
EXPERTS = 16
TOP = 4
CAP = 9
TOKENS = 384
N_EXP = 16


def level_of(rng, shape, pieces, low, top_value):
    def one(axis_at, blocks):
        draws = jax.random.uniform(jax.random.fold_in(jax.random.fold_in(rng, 6), axis_at), (blocks,), jnp.float32, low / len(pieces), top_value / len(pieces))
        return jnp.repeat(jnp.exp(draws), shape[axis_at] // blocks).reshape((-1,) + (1,) * (len(shape) - axis_at - 1))

    loudness = one(*pieces[0])
    for cut in pieces[1:]:
        loudness = loudness * one(*cut)
    return loudness


def routed_block(key, own, number, rows, count, top, bound, skew):
    order = jax.random.permutation(key, count)
    heavy_load, usual = shares(count, rows * top, bound, skew, True), shares(count, rows * top, bound, skew, False)
    places = jnp.arange(count)

    def named(lengths, offset_by):
        used = int((lengths > 0).sum())
        fixed = max(1, used // 4)
        passed = fixed + (places - fixed + offset_by * (used - fixed)) % max(1, count - fixed)
        return jnp.zeros((count,), jnp.int32).at[order[jnp.where(places < fixed, places, passed)]].set(jnp.asarray(lengths, jnp.int32))

    lengths = jnp.where(number % 4 == 0, named(heavy_load, number // 4), named(usual, number - number // 4 - 1))
    mixed = jax.random.permutation(jax.random.fold_in(own, 3), count)
    source_of, sink = mixed[0:count // 2 * 2:2], mixed[1:count // 2 * 2:2]
    slack = jnp.minimum(lengths[source_of] - 1, bound - lengths[sink]) // 2
    slack = jnp.where((source_of == order[0]) | (sink == order[0]) | (lengths[sink] == 0), 0, jnp.maximum(slack, 0))
    passed = jax.random.randint(jax.random.fold_in(own, 4), (count // 2,), 0, 1 << 20) % (slack + 1)
    lengths = lengths.at[source_of].add(-passed).at[sink].add(passed)
    members = jnp.searchsorted(jnp.cumsum(lengths), jnp.arange(rows * top), side="right").astype(jnp.int32)
    grid = members.reshape(top, rows).T
    grid = grid[jax.random.permutation(jax.random.fold_in(own, 1), rows)]
    offset_by = jax.random.randint(jax.random.fold_in(own, 2), (rows, 1), 0, top)
    return jnp.take_along_axis(grid, (jnp.arange(top)[None, :] + offset_by) % top, axis=1)


def shares(amount, total, most, lean, full):
    portions = [(1 << 20) // math.isqrt(rank ** lean) + 1 for rank in range(1, amount + 1)]
    largest = most if full else min(most, max(-(-total // amount), total * portions[0] // sum(portions)))
    least = 1 if total - largest >= amount - 1 else 0
    holding, rest = [largest] + [least] * (amount - 1), total - largest - least * (amount - 1)
    while rest > 0:
        candidates = [i for i in range(1, amount) if holding[i] < largest] or [i for i in range(1, amount) if holding[i] < most]
        pool, remaining = sum([portions[i] for i in candidates]), rest
        for i in candidates:
            more = min(most - holding[i], max(1, remaining * portions[i] // pool), rest)
            holding[i] = holding[i] + more
            rest = rest - more
    return np.array(holding)


def normal_values(stream_key, extent, deviation, most, shards=(), held_as=jnp.bfloat16):
    array = deviation * jax.random.normal(stream_key, extent, jnp.float32)
    if shards:
        array = array * level_of(stream_key, extent, shards, -0.22, 0.18)
    return jnp.clip(array, -most, most).astype(held_as)


def setup_inputs(seed: int = 0) -> dict:
    splits = jax.random.split(jax.random.key(seed), 8)
    tokens = normal_values(splits[0], (TOKENS, D), 1.0, 6.0, ((0, 16), (1, 2)))
    cotangent = normal_values(splits[1], (TOKENS, D), 1.0, 6.0, ((0, 16), (1, 2)))
    router_weight = jnp.clip(jnp.exp(math.log(0.5) - 3.224016 * jax.random.uniform(splits[2], (TOKENS, TOP), jnp.float32) ** level_of(splits[2], (TOKENS, TOP), ((0, 16),), -0.2, 0.2)), 0.019897461, 0.5).astype(jnp.bfloat16)
    expert_ids_keys = jax.random.split(jax.random.fold_in(splits[3], 1), TOKENS // TOK_DEV)
    expert_ids_turns = jax.random.permutation(jax.random.fold_in(splits[3], 3), TOKENS // TOK_DEV)
    expert_ids = jax.vmap(lambda own, number: routed_block(jax.random.fold_in(splits[3], 2), own, number, TOK_DEV, EXPERTS, TOP, CAP, 2))(expert_ids_keys, expert_ids_turns).reshape((TOKENS, TOP))
    w_gate = normal_values(splits[4], (EXPERTS, D, FF), D ** -0.5, 0.125, ((0, 16), (1, 2)))
    w_up = normal_values(splits[5], (EXPERTS, D, FF), D ** -0.5, 0.125, ((0, 16), (1, 2)))
    w_down = normal_values(splits[6], (EXPERTS, FF, D), FF ** -0.5, 0.21875, ((0, 16), (2, 2)))
    return {"tokens": tokens, "cotangent": cotangent, "router_weight": router_weight, "expert_ids": expert_ids, "w_gate": w_gate, "w_up": w_up, "w_down": w_down}


def slot_layout(expert_ids):
    token_count = expert_ids.shape[0]
    expert_range = jnp.arange(EXPERTS, dtype=jnp.int32)
    per_token = jnp.sum((expert_ids[:, :, None] == expert_range[None, None, :]).astype(jnp.int32), axis=1)
    blocked = per_token.reshape(N_EXP, TOK_DEV, EXPERTS)
    earlier = (jnp.cumsum(blocked, axis=1) - blocked).reshape(token_count, EXPERTS)
    ranking = jnp.take_along_axis(earlier, expert_ids, axis=1).astype(jnp.int32)
    source = (jnp.arange(token_count, dtype=jnp.int32) // TOK_DEV).astype(jnp.int32)
    return (source[:, None] * CAP + ranking).astype(jnp.int32)


def expert_pass(tokens, cotangent, table_rows, table_weights, gate_mat, up_mat, down_mat):
    valid = table_rows >= 0
    safe_rows = jnp.maximum(table_rows, 0).astype(jnp.int32)
    inputs = jnp.where(valid[:, None], tokens[safe_rows], jnp.zeros((), tokens.dtype))
    upstream = jnp.where(valid[:, None], cotangent[safe_rows], jnp.zeros((), cotangent.dtype))
    gate = jnp.dot(inputs, gate_mat, preferred_element_type=jnp.float32)
    upval = jnp.dot(inputs, up_mat, preferred_element_type=jnp.float32)
    active = jax.nn.silu(gate)
    hidden = (active * upval).astype(jnp.bfloat16)
    outputs = jnp.dot(hidden, down_mat, preferred_element_type=jnp.float32).astype(jnp.bfloat16)
    out_delta = (table_weights[:, None] * upstream.astype(jnp.float32)).astype(jnp.bfloat16)
    hidden_delta = jnp.dot(out_delta, down_mat.T, preferred_element_type=jnp.float32)
    sigmoid = jax.nn.sigmoid(gate)
    gate_delta = (hidden_delta * upval * sigmoid * (1.0 + gate * (1.0 - sigmoid))).astype(jnp.bfloat16)
    up_delta = (hidden_delta * active).astype(jnp.bfloat16)
    down_grad = jnp.dot(hidden.T, out_delta, preferred_element_type=jnp.float32).astype(jnp.bfloat16)
    gate_grad = jnp.dot(inputs.T, gate_delta, preferred_element_type=jnp.float32).astype(jnp.bfloat16)
    up_grad = jnp.dot(inputs.T, up_delta, preferred_element_type=jnp.float32).astype(jnp.bfloat16)
    token_delta = (jnp.dot(gate_delta, gate_mat.T, preferred_element_type=jnp.float32)
                   + jnp.dot(up_delta, up_mat.T, preferred_element_type=jnp.float32)).astype(jnp.bfloat16)
    return outputs, token_delta, gate_grad, up_grad, down_grad


def reference(tokens, cotangent, router_weight, expert_ids, w_gate, w_up, w_down):
    token_count = tokens.shape[0]
    slot_pos = slot_layout(expert_ids)
    token_index = jnp.broadcast_to(jnp.arange(token_count, dtype=jnp.int32)[:, None], expert_ids.shape)
    table = jnp.full((EXPERTS, N_EXP * CAP), -1, jnp.int32).at[expert_ids, slot_pos].set(token_index)
    weight_table = jnp.zeros((EXPERTS, N_EXP * CAP), jnp.float32).at[expert_ids, slot_pos].set(
        router_weight.astype(jnp.float32))

    def one_expert(packed):
        table_rows, table_weights, gate_mat, up_mat, down_mat = packed
        return expert_pass(tokens, cotangent, table_rows, table_weights, gate_mat, up_mat, down_mat)

    outputs, token_delta, gate_grad, up_grad, down_grad = lax.map(
        one_expert, (table, weight_table, w_gate, w_up, w_down))
    route_out = outputs[expert_ids, slot_pos].astype(jnp.float32)
    route_delta = token_delta[expert_ids, slot_pos].astype(jnp.float32)
    weights = router_weight.astype(jnp.float32)
    mixed = jnp.sum(weights[:, :, None] * route_out, axis=1).astype(jnp.bfloat16)
    router_grad = jnp.sum(route_out * cotangent.astype(jnp.float32)[:, None, :], axis=2).astype(jnp.bfloat16)
    token_grad = jnp.sum(route_delta, axis=1).astype(jnp.bfloat16)
    return mixed, token_grad, router_grad, gate_grad, up_grad, down_grad
```

```python
import functools
import math

import jax
import jax.numpy as jnp
from jax import lax
from jax.experimental import pallas as pl
from jax.experimental.pallas import tpu as pltpu
from jax.sharding import PartitionSpec as P

MESH = pl.DeviceIdType.MESH
F32 = jnp.float32
BF16 = jnp.bfloat16
META = 128
SLOT_LANE, WEIGHT_LANE, HALF_LANE = 16, 32, 48


def factors(n):
    nc = 2
    chips = n // nc
    ny = 1 << (int(math.log2(chips)) // 2)
    return chips // ny, ny, nc


def dot(a, b):
    return lax.dot_general(a, b, (((1,), (0,)), ((), ())), preferred_element_type=F32)


def dot_tn(a, b):
    return lax.dot_general(a, b, (((0,), (0,)), ((), ())), preferred_element_type=F32)


def dot_nt(a, b):
    return lax.dot_general(a, b, (((1,), (1,)), ((), ())), preferred_element_type=F32)


def kernel(
    shape, tok, cot, rw, ids, wg_hbm, wu_hbm, wd_hbm,
    mixed, tgrad, rgrad, gg_hbm, ug_hbm, dg_hbm,
    wg, wu, wd, gg, ug, dg,
    abuf, bbuf, st, xs, us, xb,
    rm, rm_c, am1, rm_y, am2, rm_z,
    rd, rd_c, ad1, rd_y, ad2, rd_z,
    wsem, osem, ag_send, ag_recv, x_send, x_recv, rs_send, rs_recv,
):
    nz, ny, nc, nr, cap, chunks = shape
    n = nz * ny * nc
    total = n * cap
    rows, top = ids.shape
    width = tok.shape[1]
    half = width // 2
    ff = wg.shape[1]

    me_r = lax.axis_index("rep")
    me = lax.axis_index("exp")
    z = me // (ny * nc)
    y = (me // nc) % ny
    c = me % nc

    def exp_at(zz, yy, cc):
        return (me_r, (zz * ny + yy) * nc + cc)

    z_peers = [exp_at((z + d) % nz, y, c) for d in range(1, nz)]
    y_peers = [exp_at(z, (y + d) % ny, c) for d in range(1, ny)]
    c_peers = [exp_at(z, y, (c + d) % nc) for d in range(1, nc)]
    r_peers = [((me_r + d) % nr, me) for d in range(1, nr)]
    everyone = z_peers + y_peers + c_peers + r_peers

    barrier = pltpu.get_barrier_semaphore()
    for peer in everyone:
        pl.semaphore_signal(barrier, inc=1, device_id=peer, device_id_type=MESH)

    loads = [
        pltpu.make_async_copy(src, dst, wsem.at[i])
        for i, (src, dst) in enumerate(((wg_hbm, wg), (wu_hbm, wu), (wd_hbm, wd)))
    ]
    for load in loads:
        load.start()

    lane = lax.broadcasted_iota(jnp.int32, (rows, META), 1)
    own_ids = ids[...]
    own_w = rw[...].astype(F32)
    named = jnp.zeros((rows, META), F32)
    for k in range(top):
        named += (own_ids[:, k:k + 1] == lane).astype(F32)
    before = (
        lax.broadcasted_iota(jnp.int32, (rows, rows), 1)
        < lax.broadcasted_iota(jnp.int32, (rows, rows), 0)
    ).astype(F32)
    earlier = dot(before, named)
    meta = jnp.zeros((rows, META), F32)
    first_slot = (me * cap).astype(F32)
    for k in range(top):
        id_k = own_ids[:, k:k + 1]
        rank = jnp.sum(jnp.where(id_k == lane, earlier, 0.0), axis=1, keepdims=True)
        meta = jnp.where(lane == k, id_k.astype(F32), meta)
        meta = jnp.where(lane == SLOT_LANE + k, rank + first_slot, meta)
        meta = jnp.where(lane == WEIGHT_LANE + k, own_w[:, k:k + 1], meta)
    tok_v = tok[...].astype(F32)
    cot_v = cot[...].astype(F32)
    abuf[z, y, c, :, :half] = jnp.concatenate(
        [tok_v[:, :half], tok_v[:, half:]], axis=0).astype(BF16)
    abuf[z, y, c, :, half:] = jnp.concatenate(
        [meta, jnp.where(lane == HALF_LANE, 1.0, meta)], axis=0).astype(BF16)
    bbuf[z, y, c] = jnp.concatenate(
        [cot_v[:, :half], cot_v[:, half:]], axis=0).astype(BF16)

    pl.semaphore_wait(barrier, len(everyone))

    sends = []

    def send(src, dst, s_sem, r_sem, peer):
        copy = pltpu.make_async_remote_copy(
            src_ref=src, dst_ref=dst, send_sem=s_sem, recv_sem=r_sem,
            device_id=peer, device_id_type=MESH)
        copy.start()
        sends.append(copy)
        return copy

    def gather_stage(buf, which, stage, peers, view):
        return [
            send(view(buf), view(buf), ag_send.at[which, stage, d],
                 ag_recv.at[which, stage, d], peer)
            for d, peer in enumerate(peers)
        ]

    def arrive(copies):
        for copy in copies:
            copy.wait_recv()

    def at_z(buf):
        return buf.at[z, y, c]

    def at_y(buf):
        return buf.at[:, y, c]

    def at_c(buf):
        return buf.at[:, :, c]

    a_z = gather_stage(abuf, 0, 0, z_peers, at_z)
    arrive(a_z)
    a_y = gather_stage(abuf, 0, 1, y_peers, at_y)
    b_z = gather_stage(bbuf, 1, 0, z_peers, at_z)
    arrive(a_y)
    a_c = gather_stage(abuf, 0, 2, c_peers, at_c)
    arrive(b_z)
    b_y = gather_stage(bbuf, 1, 1, y_peers, at_y)
    arrive(a_c)

    zs = nz // chunks
    per = zs * ny * nc * 2 * rows

    def build(i, acc):
        part = abuf[pl.ds(i * zs, zs)].reshape(per, half + META)
        info = part[:, half:].astype(F32)
        lanes = lax.broadcasted_iota(jnp.int32, (per, META), 1)
        match = (info == me.astype(F32)) & (lanes < top)
        slot = jnp.sum(
            jnp.where(match, pltpu.roll(info, META - SLOT_LANE, 1), 0.0)
            + jnp.where(lanes == HALF_LANE, info * total, 0.0),
            axis=1, keepdims=True)
        found = jnp.sum(match.astype(F32), axis=1, keepdims=True)
        slot = jnp.where(found > 0.0, slot, -1.0).astype(jnp.int32)
        place = lax.broadcasted_iota(jnp.int32, (per, 2 * total), 1) == slot
        placed = jnp.where(place, 1.0, 0.0).astype(BF16)
        st[i] = placed
        return acc + dot_tn(placed, part)

    def over_chunks(body, start):
        if chunks == 1:
            return body(0, start)
        return lax.fori_loop(0, chunks, body, start)

    gathered = over_chunks(build, jnp.zeros((2 * total, half + META), F32))
    xs[...] = gathered[:, :half].astype(BF16)
    info = gathered[:total, half:]
    lanes = lax.broadcasted_iota(jnp.int32, (total, META), 1)
    match = (info == me.astype(F32)) & (lanes < top)
    slot_w = jnp.sum(
        jnp.where(match, pltpu.roll(info, META - WEIGHT_LANE, 1), 0.0), axis=1, keepdims=True)

    def exchange(i, value):
        xb[me_r, i] = value.astype(BF16)
        return [
            send(xb.at[me_r, i], xb.at[me_r, i], x_send.at[i, d], x_recv.at[i, d], peer)
            for d, peer in enumerate(r_peers)
        ]

    def summed(i):
        value = xb[0, i].astype(F32)
        for r in range(1, nr):
            value = value + xb[r, i].astype(F32)
        return value

    loads[0].wait()
    x_gate = exchange(0, dot(xs[:total], wg[:half]) + dot(xs[total:], wg[half:]))
    loads[1].wait()
    x_up = exchange(1, dot(xs[:total], wu[:half]) + dot(xs[total:], wu[half:]))

    arrive(b_y)
    b_c = gather_stage(bbuf, 1, 2, c_peers, at_c)
    arrive(b_c)

    def take(i, acc):
        part = bbuf[pl.ds(i * zs, zs)].reshape(per, half)
        return acc + dot_tn(st[i], part)

    us[...] = over_chunks(take, jnp.zeros((2 * total, half), F32)).astype(BF16)
    loads[2].wait()
    x_hid = exchange(2, dot_nt(us[:total], wd[:, :half]) + dot_nt(us[total:], wd[:, half:]))

    us[:total] = (slot_w * us[:total].astype(F32)).astype(BF16)
    us[total:] = (slot_w * us[total:].astype(F32)).astype(BF16)

    def scatter_core(buf, got, which):
        return [
            send(buf.at[:, :, (c + d + 1) % nc], got.at[d], rs_send.at[which, 0, d],
                 rs_recv.at[which, 0, d], peer)
            for d, peer in enumerate(c_peers)
        ]

    def scatter_y(buf, got, which):
        return [
            send(buf.at[:, (y + d + 1) % ny], got.at[d], rs_send.at[which, 1, d],
                 rs_recv.at[which, 1, d], peer)
            for d, peer in enumerate(y_peers)
        ]

    def scatter_z(buf, got, which):
        return [
            send(buf.at[(z + d + 1) % nz], got.at[d], rs_send.at[which, 2, d],
                 rs_recv.at[which, 2, d], peer)
            for d, peer in enumerate(z_peers)
        ]

    def added(own, got, count):
        value = own.astype(F32)
        for d in range(count):
            value = value + got[d].astype(F32)
        return value

    arrive(x_gate)
    arrive(x_up)
    gate = summed(0)
    up = summed(1)
    sig = 1.0 / (1.0 + jnp.exp(-gate))
    active = gate * sig
    hidden32 = active * up
    hidden = hidden32.astype(BF16)

    def weighted(value):
        return (slot_w * value.astype(BF16).astype(F32)).astype(BF16)

    out = jnp.concatenate(
        [weighted(dot(hidden, wd[:, :half])), weighted(dot(hidden, wd[:, half:]))], axis=0)

    def spread_out(i, acc):
        rm[pl.ds(i * zs, zs)] = dot(st[i], out).astype(BF16).reshape(
            zs, ny, nc, 2 * rows, half)
        return acc

    over_chunks(spread_out, 0)
    m_c = scatter_core(rm, rm_c, 0)

    arrive(x_hid)
    hid_plain = summed(2)
    router = jnp.sum(hidden.astype(F32) * hid_plain, axis=1, keepdims=True)
    hid = slot_w * hid_plain
    gate_delta = (hid * up * sig * (1.0 + gate * (1.0 - sig))).astype(BF16)
    up_delta = (hid * active).astype(BF16)
    delta = jnp.concatenate(
        [(dot_nt(gate_delta, wg[:half]) + dot_nt(up_delta, wu[:half])).astype(BF16),
         (dot_nt(gate_delta, wg[half:]) + dot_nt(up_delta, wu[half:])).astype(BF16)], axis=0)
    router_wide = jnp.concatenate(
        [jnp.broadcast_to(router, (total, META)), jnp.zeros((total, META), F32)],
        axis=0).astype(BF16)

    def spread_delta(i, acc):
        rd[pl.ds(i * zs, zs), :, :, :, :half] = dot(st[i], delta).astype(BF16).reshape(
            zs, ny, nc, 2 * rows, half)
        info_i = abuf[pl.ds(i * zs, zs), :, :, :, half:].reshape(per, META).astype(F32)
        lanes_i = lax.broadcasted_iota(jnp.int32, (per, META), 1)
        hit = (info_i == me.astype(F32)) & (lanes_i < top)
        rd[pl.ds(i * zs, zs), :, :, :, half:] = jnp.where(
            hit, dot(st[i], router_wide), 0.0).astype(BF16).reshape(
                zs, ny, nc, 2 * rows, META)
        return acc

    over_chunks(spread_delta, 0)
    d_c = scatter_core(rd, rd_c, 1)

    stores = []

    def store(src, dst, i):
        copy = pltpu.make_async_copy(src, dst, osem.at[i])
        copy.start()
        stores.append(copy)

    arrive(m_c)
    am1[...] = added(rm[:, :, c], rm_c, nc - 1).astype(BF16)
    m_y = scatter_y(am1, rm_y, 0)

    dg[:, :half] = dot_tn(hidden, us[:total]).astype(BF16)

    arrive(d_c)
    ad1[...] = added(rd[:, :, c], rd_c, nc - 1).astype(BF16)
    d_y = scatter_y(ad1, rd_y, 1)

    dg[:, half:] = dot_tn(hidden, us[total:]).astype(BF16)
    store(dg, dg_hbm, 0)

    arrive(m_y)
    am2[...] = added(am1[:, y], rm_y, ny - 1).astype(BF16)
    m_z = scatter_z(am2, rm_z, 0)

    gg[:half] = dot_tn(xs[:total], gate_delta).astype(BF16)
    gg[half:] = dot_tn(xs[total:], gate_delta).astype(BF16)
    store(gg, gg_hbm, 1)

    arrive(d_y)
    ad2[...] = added(ad1[:, y], rd_y, ny - 1).astype(BF16)
    d_z = scatter_z(ad2, rd_z, 1)

    ug[:half] = dot_tn(xs[:total], up_delta).astype(BF16)
    ug[half:] = dot_tn(xs[total:], up_delta).astype(BF16)
    store(ug, ug_hbm, 2)

    arrive(m_z)
    value = added(am2[z], rm_z, nz - 1)
    mixed[:, :half] = value[:rows].astype(BF16)
    mixed[:, half:] = value[rows:].astype(BF16)
    arrive(d_z)
    value = added(ad2[z], rd_z, nz - 1)
    tgrad[:, :half] = value[:rows, :half].astype(BF16)
    tgrad[:, half:] = value[rows:, :half].astype(BF16)
    rgrad[...] = value[:rows, half:half + top].astype(BF16)

    for copy in sends:
        copy.wait_send()
    for copy in stores:
        copy.wait()


def local(shape, tokens, cotangent, router_weight, expert_ids, w_gate, w_up, w_down):
    nz, ny, nc, nr, cap, chunks = shape
    n = nz * ny * nc
    total = n * cap
    rows, top = expert_ids.shape
    width = tokens.shape[1]
    half = width // 2
    ff = w_gate.shape[2]
    tall = 2 * rows
    wide = half + META
    per = n // chunks * tall
    deep = max(nz, ny, nc) - 1
    vmem = pl.BlockSpec(memory_space=pltpu.VMEM)
    anywhere = pl.BlockSpec(memory_space=pl.ANY)
    v = pltpu.VMEM

    def scatter_buffers(w):
        return [
            v((nz, ny, nc, tall, w), BF16),
            v((nc - 1, nz, ny, tall, w), BF16),
            v((nz, ny, tall, w), BF16),
            v((ny - 1, nz, tall, w), BF16),
            v((nz, tall, w), BF16),
            v((nz - 1, tall, w), BF16),
        ]

    dma = pltpu.SemaphoreType.DMA
    flops = 2 * 9 * total * width * ff
    mixed, tgrad, rgrad, gg, ug, dg = pl.pallas_call(
        functools.partial(kernel, shape),
        out_shape=(
            jax.ShapeDtypeStruct((rows, width), BF16),
            jax.ShapeDtypeStruct((rows, width), BF16),
            jax.ShapeDtypeStruct((rows, top), BF16),
            jax.ShapeDtypeStruct((width, ff), BF16),
            jax.ShapeDtypeStruct((width, ff), BF16),
            jax.ShapeDtypeStruct((ff, width), BF16),
        ),
        in_specs=[vmem] * 4 + [anywhere] * 3,
        out_specs=(vmem,) * 3 + (anywhere,) * 3,
        scratch_shapes=[
            v((width, ff), BF16), v((width, ff), BF16), v((ff, width), BF16),
            v((width, ff), BF16), v((width, ff), BF16), v((ff, width), BF16),
            v((nz, ny, nc, tall, wide), BF16),
            v((nz, ny, nc, tall, half), BF16),
            v((chunks, per, 2 * total), BF16),
            v((2 * total, half), BF16),
            v((2 * total, half), BF16),
            v((nr, 3, total, ff), BF16),
            *scatter_buffers(half),
            *scatter_buffers(wide),
            dma((3,)), dma((3,)),
            dma((2, 3, deep)), dma((2, 3, deep)),
            dma((3, nr - 1)), dma((3, nr - 1)),
            dma((2, 3, deep)), dma((2, 3, deep)),
        ],
        compiler_params=pltpu.CompilerParams(
            collective_id=0, has_side_effects=True, vmem_limit_bytes=60 * 1024 * 1024),
        cost_estimate=pl.CostEstimate(
            flops=flops, bytes_accessed=12 * width * ff, transcendentals=total * ff),
    )(tokens, cotangent, router_weight, expert_ids, w_gate[0], w_up[0], w_down[0])
    return (mixed, tgrad, rgrad, gg[None], ug[None], dg[None])


def solution(mesh):
    n = mesh.shape["exp"]
    nr = mesh.shape["rep"]

    def step(tokens, cotangent, router_weight, expert_ids, w_gate, w_up, w_down):
        rows, top = expert_ids.shape
        cap = min(rows, max(2, rows * top * 3 // (2 * n)))
        nz, ny, nc = factors(n)
        chunks = max(1, n * 2 * rows // 768)
        while nz % chunks:
            chunks -= 1
        return local(
            (nz, ny, nc, nr, cap, chunks),
            tokens, cotangent, router_weight, expert_ids, w_gate, w_up, w_down)

    return jax.shard_map(
        step,
        mesh=mesh,
        in_specs=(
            P("exp", "rep"),
            P("exp", "rep"),
            P("exp", None),
            P("exp", None),
            P("exp", "rep", None),
            P("exp", "rep", None),
            P("exp", None, "rep"),
        ),
        out_specs=(
            P("exp", "rep"),
            P("exp", "rep"),
            P("exp", None),
            P("exp", "rep", None),
            P("exp", "rep", None),
            P("exp", None, "rep"),
        ),
        check_vma=False,
    )
```

```python
import functools
import math

import jax
import jax.numpy as jnp
from jax import lax
from jax.experimental import pallas as pl
from jax.experimental.pallas import tpu as pltpu
from jax.sharding import PartitionSpec as P

MESH = pl.DeviceIdType.MESH
F32 = jnp.float32
BF16 = jnp.bfloat16
META = 128
SLOT_LANE, WEIGHT_LANE, HALF_LANE = 16, 32, 48


def factors(n):
    nc = 2
    chips = n // nc
    ny = 1 << (int(math.log2(chips)) // 2)
    return chips // ny, ny, nc


def dot(a, b):
    return lax.dot_general(a, b, (((1,), (0,)), ((), ())), preferred_element_type=F32)


def dot_tn(a, b):
    return lax.dot_general(a, b, (((0,), (0,)), ((), ())), preferred_element_type=F32)


def dot_nt(a, b):
    return lax.dot_general(a, b, (((1,), (1,)), ((), ())), preferred_element_type=F32)


def kernel(
    shape, tok, cot, rw, ids, wg_hbm, wu_hbm, wd_hbm,
    mixed, tgrad, rgrad, xs, us, hid_out, gd_out, ud_out,
    wg, wu, wd, abuf, bbuf, st, xb,
    rm, rm_c, am1, rm_y, am2, rm_z,
    rd, rd_c, ad1, rd_y, ad2, rd_z,
    wsem, ag_send, ag_recv, x_send, x_recv, rs_send, rs_recv,
):
    nz, ny, nc, nr, cap, chunks = shape
    n = nz * ny * nc
    total = n * cap
    top, rows = ids.shape
    width = tok.shape[1]
    half = width // 2

    me_r = lax.axis_index("rep")
    me = lax.axis_index("exp")
    z = me // (ny * nc)
    y = (me // nc) % ny
    c = me % nc

    def exp_at(zz, yy, cc):
        return (me_r, (zz * ny + yy) * nc + cc)

    z_peers = [exp_at((z + d) % nz, y, c) for d in range(1, nz)]
    y_peers = [exp_at(z, (y + d) % ny, c) for d in range(1, ny)]
    c_peers = [exp_at(z, y, (c + d) % nc) for d in range(1, nc)]
    r_peers = [((me_r + d) % nr, me) for d in range(1, nr)]
    everyone = z_peers + y_peers + c_peers + r_peers

    barrier = pltpu.get_barrier_semaphore()
    for peer in everyone:
        pl.semaphore_signal(barrier, inc=1, device_id=peer, device_id_type=MESH)

    loads = [
        pltpu.make_async_copy(src, dst, wsem.at[i])
        for i, (src, dst) in enumerate(((wg_hbm, wg), (wu_hbm, wu), (wd_hbm, wd)))
    ]
    for load in loads:
        load.start()

    lane = lax.broadcasted_iota(jnp.int32, (rows, META), 1)
    spot = lax.broadcasted_iota(jnp.int32, (top, META), 1)
    which_k = lax.broadcasted_iota(jnp.int32, (top, META), 0)

    def columns(value, at):
        return dot_tn(value.astype(F32), (spot == which_k + at).astype(F32))

    own_ids = columns(ids[...], 0)
    lane_f = lane.astype(F32)
    named = jnp.zeros((rows, META), F32)
    for k in range(top):
        named += (own_ids[:, k:k + 1] == lane_f).astype(F32)
    before = (
        lax.broadcasted_iota(jnp.int32, (rows, rows), 1)
        < lax.broadcasted_iota(jnp.int32, (rows, rows), 0)
    ).astype(F32)
    earlier = dot(before, named)
    meta = own_ids + columns(rw[...], WEIGHT_LANE)
    first_slot = (me * cap).astype(F32)
    for k in range(top):
        id_k = own_ids[:, k:k + 1]
        rank = jnp.sum(jnp.where(id_k == lane_f, earlier, 0.0), axis=1, keepdims=True)
        meta = jnp.where(lane == SLOT_LANE + k, rank + first_slot, meta)
    tok_v = tok[...].astype(F32)
    cot_v = cot[...].astype(F32)
    abuf[z, y, c, :, :half] = jnp.concatenate(
        [tok_v[:, :half], tok_v[:, half:]], axis=0).astype(BF16)
    abuf[z, y, c, :, half:] = jnp.concatenate(
        [meta, jnp.where(lane == HALF_LANE, 1.0, meta)], axis=0).astype(BF16)
    bbuf[z, y, c] = jnp.concatenate(
        [cot_v[:, :half], cot_v[:, half:]], axis=0).astype(BF16)

    pl.semaphore_wait(barrier, len(everyone))

    sends = []

    def send(src, dst, s_sem, r_sem, peer):
        copy = pltpu.make_async_remote_copy(
            src_ref=src, dst_ref=dst, send_sem=s_sem, recv_sem=r_sem,
            device_id=peer, device_id_type=MESH)
        copy.start()
        sends.append(copy)
        return copy

    def arrive(copies):
        for copy in copies:
            copy.wait_recv()

    def gather(buf, which):
        def move(zz, yy, slot, peer):
            block = buf.at[zz, yy, c] if yy is not None else buf.at[zz, y, c]
            return pltpu.make_async_remote_copy(
                src_ref=block, dst_ref=block, send_sem=ag_send.at[which, slot],
                recv_sem=ag_recv.at[which, slot], device_id=peer, device_id_type=MESH)

        up_to = exp_at(jnp.minimum(z + 1, nz - 1), y, c)
        down_to = exp_at(jnp.maximum(z - 1, 0), y, c)
        base_y = 2 * nz
        base_c = base_y + 2 * nz * (ny - 1)

        def over_y(zz, tag):
            return [
                move(zz, y, base_y + tag * (ny - 1) + e, peer)
                for e, peer in enumerate(y_peers)
            ]

        def over_c(zz, tag, some):
            found = []
            for e in some:
                for f, peer in enumerate(c_peers):
                    slot = base_c + (tag * ny + e) * (nc - 1) + f
                    found.append(move(zz, (y + ny - e) % ny, slot, peer))
            return found

        steps = []
        for s in range(nz):
            if s == 0:
                steps.append((0, z, None))
            else:
                steps.append((s, jnp.maximum(z - s, 0), z >= s))
                steps.append((nz + s, jnp.minimum(z + s, nz - 1), z + s < nz))

        def guarded(cond, body):
            if cond is None:
                body()
            else:
                pl.when(cond)(body)

        def links(tag, zz, cond, act):
            own = tag == 0
            if own or tag < nz:
                s = tag
                if s + 1 < nz:
                    more = z + 1 < nz if own else (z >= s) & (z + 1 < nz)
                    guarded(more, lambda: act(move(zz, y, s + 1, up_to)))
            if own or tag > nz:
                s = 0 if own else tag - nz
                if s + 1 < nz:
                    more = z >= 1 if own else (z + s < nz) & (z >= 1)
                    guarded(more, lambda: act(move(zz, y, nz + s + 1, down_to)))

        def begin(tag, zz, cond):
            def body():
                if tag != 0:
                    move(zz, y, tag, up_to).wait_recv()

            guarded(cond, body)
            links(tag, zz, cond, lambda copy: copy.start())

            def rest():
                for copy in over_y(zz, tag):
                    copy.start()
                for copy in over_c(zz, tag, [0]):
                    copy.start()

            guarded(cond, rest)

        def pass_on(tag, zz, cond):
            def body():
                for e, copy in enumerate(over_y(zz, tag)):
                    copy.wait_recv()
                    for onward in over_c(zz, tag, [e + 1]):
                        onward.start()

            guarded(cond, body)

        def finish(tag, zz, cond):
            def body():
                for copy in over_c(zz, tag, range(ny)):
                    copy.wait_recv()

            guarded(cond, body)

        def drain():
            for tag, zz, cond in steps:
                links(tag, zz, cond, lambda copy: copy.wait_send())

                def body(zz=zz, tag=tag):
                    for copy in over_y(zz, tag) + over_c(zz, tag, range(ny)):
                        copy.wait_send()

                guarded(cond, body)

        def first():
            begin(*steps[0])

        def middle(part, parts):
            count = len(steps) - 1
            for i in range(part * count // parts, (part + 1) * count // parts):
                begin(*steps[i + 1])
                pass_on(*steps[i])

        def last():
            pass_on(*steps[-1])
            for step in steps:
                finish(*step)

        return first, middle, last, drain

    a_first, a_middle, a_last, a_drain = gather(abuf, 0)
    b_first, b_middle, b_last, b_drain = gather(bbuf, 1)
    a_first()
    a_middle(0, 1)
    b_first()
    a_last()

    zs = nz // chunks
    per = zs * ny * nc * 2 * rows

    def build(i, acc):
        part = abuf[pl.ds(i * zs, zs)].reshape(per, half + META)
        info = part[:, half:].astype(F32)
        lanes = lax.broadcasted_iota(jnp.int32, (per, META), 1)
        match = (info == me.astype(F32)) & (lanes < top)
        slot = jnp.sum(
            jnp.where(match, pltpu.roll(info, META - SLOT_LANE, 1), 0.0)
            + jnp.where(lanes == HALF_LANE, info * total, 0.0),
            axis=1, keepdims=True)
        found = jnp.sum(match.astype(F32), axis=1, keepdims=True)
        slot = jnp.where(found > 0.0, slot, -1.0).astype(jnp.int32)
        place = lax.broadcasted_iota(jnp.int32, (per, 2 * total), 1) == slot
        placed = jnp.where(place, 1.0, 0.0).astype(BF16)
        st[i] = placed
        return acc + dot_tn(placed, part)

    def over_chunks(body, start):
        if chunks == 1:
            return body(0, start)
        return lax.fori_loop(0, chunks, body, start)

    gathered = over_chunks(build, jnp.zeros((2 * total, half + META), F32))
    xs[0] = gathered[:total, :half].astype(BF16)
    xs[1] = gathered[total:, :half].astype(BF16)
    info = gathered[:total, half:]
    lanes = lax.broadcasted_iota(jnp.int32, (total, META), 1)
    match = (info == me.astype(F32)) & (lanes < top)
    slot_w = jnp.sum(
        jnp.where(match, pltpu.roll(info, META - WEIGHT_LANE, 1), 0.0), axis=1, keepdims=True)

    b_middle(0, 3)

    def exchange(i, value):
        xb[me_r, i] = value.astype(BF16)
        return [
            send(xb.at[me_r, i], xb.at[me_r, i], x_send.at[i, d], x_recv.at[i, d], peer)
            for d, peer in enumerate(r_peers)
        ]

    def summed(i):
        value = xb[0, i].astype(F32)
        for r in range(1, nr):
            value = value + xb[r, i].astype(F32)
        return value

    loads[0].wait()
    x_gate = exchange(0, dot(xs[0], wg[:half]) + dot(xs[1], wg[half:]))
    b_middle(1, 3)
    loads[1].wait()
    x_up = exchange(1, dot(xs[0], wu[:half]) + dot(xs[1], wu[half:]))

    b_middle(2, 3)
    b_last()

    def take(i, acc):
        part = bbuf[pl.ds(i * zs, zs)].reshape(per, half)
        return acc + dot_tn(st[i], part)

    upstream = over_chunks(take, jnp.zeros((2 * total, half), F32))
    up_left = upstream[:total].astype(BF16)
    up_right = upstream[total:].astype(BF16)
    loads[2].wait()
    x_hid = exchange(2, dot_nt(up_left, wd[:, :half]) + dot_nt(up_right, wd[:, half:]))
    us[0] = (slot_w * up_left.astype(F32)).astype(BF16)
    us[1] = (slot_w * up_right.astype(F32)).astype(BF16)

    def dest(j):
        return (z + j + 1) % nz

    def scatter_core(buf, got, which):
        return [
            [
                send(buf.at[dest(j), :, (c + d + 1) % nc], got.at[d, dest(j)],
                     rs_send.at[which, 0, j, d], rs_recv.at[which, 0, j, d], peer)
                for d, peer in enumerate(c_peers)
            ]
            for j in range(nz)
        ]

    def scatter_y(copies, buf, got, summed_c, got_y, which):
        on = []
        for j in range(nz):
            arrive(copies[j])
            zz = dest(j)
            value = buf[zz, :, c].astype(F32)
            for d in range(nc - 1):
                value = value + got[d, zz].astype(F32)
            summed_c[zz] = value.astype(BF16)
            on.append([
                send(summed_c.at[zz, (y + d + 1) % ny], got_y.at[d, zz],
                     rs_send.at[which, 1, j, d], rs_recv.at[which, 1, j, d], peer)
                for d, peer in enumerate(y_peers)
            ])
        return on

    def scatter_z(copies, summed_c, got_y, summed_y, got_z, which):
        on = []
        for j in range(nz):
            arrive(copies[j])
            zz = dest(j)
            value = summed_c[zz, y].astype(F32)
            for d in range(ny - 1):
                value = value + got_y[d, zz].astype(F32)
            summed_y[zz] = value.astype(BF16)
            if j < nz - 1:
                on.append(
                    send(summed_y.at[zz], got_z.at[j], rs_send.at[which, 2, j, 0],
                         rs_recv.at[which, 2, j, 0], z_peers[j]))
        return on

    def added(own, got, count):
        value = own.astype(F32)
        for d in range(count):
            value = value + got[d].astype(F32)
        return value

    arrive(x_gate)
    arrive(x_up)
    gate = summed(0)
    up = summed(1)
    sig = 1.0 / (1.0 + jnp.exp(-gate))
    active = gate * sig
    hidden32 = active * up
    hidden = hidden32.astype(BF16)

    def weighted(value):
        return (slot_w * value.astype(BF16).astype(F32)).astype(BF16)

    out = jnp.concatenate(
        [weighted(dot(hidden, wd[:, :half])), weighted(dot(hidden, wd[:, half:]))], axis=0)

    def spread_out(i, acc):
        rm[pl.ds(i * zs, zs)] = dot(st[i], out).astype(BF16).reshape(
            zs, ny, nc, 2 * rows, half)
        return acc

    over_chunks(spread_out, 0)
    m_c = scatter_core(rm, rm_c, 0)
    hid_out[...] = hidden
    m_y = scatter_y(m_c, rm, rm_c, am1, rm_y, 0)

    arrive(x_hid)
    hid_plain = summed(2)
    router = jnp.sum(hidden.astype(F32) * hid_plain, axis=1, keepdims=True)
    hid = slot_w * hid_plain
    gate_delta = (hid * up * sig * (1.0 + gate * (1.0 - sig))).astype(BF16)
    up_delta = (hid * active).astype(BF16)
    delta = jnp.concatenate(
        [(dot_nt(gate_delta, wg[:half]) + dot_nt(up_delta, wu[:half])).astype(BF16),
         (dot_nt(gate_delta, wg[half:]) + dot_nt(up_delta, wu[half:])).astype(BF16)], axis=0)
    router_wide = jnp.concatenate(
        [jnp.broadcast_to(router, (total, META)), jnp.zeros((total, META), F32)],
        axis=0).astype(BF16)

    def spread_delta(i, acc):
        rd[pl.ds(i * zs, zs), :, :, :, :half] = dot(st[i], delta).astype(BF16).reshape(
            zs, ny, nc, 2 * rows, half)
        info_i = abuf[pl.ds(i * zs, zs), :, :, :, half:].reshape(per, META).astype(F32)
        lanes_i = lax.broadcasted_iota(jnp.int32, (per, META), 1)
        hit = (info_i == me.astype(F32)) & (lanes_i < top)
        rd[pl.ds(i * zs, zs), :, :, :, half:] = jnp.where(
            hit, dot(st[i], router_wide), 0.0).astype(BF16).reshape(
                zs, ny, nc, 2 * rows, META)
        return acc

    over_chunks(spread_delta, 0)
    d_c = scatter_core(rd, rd_c, 1)

    gd_out[...] = gate_delta
    ud_out[...] = up_delta
    m_z = scatter_z(m_y, am1, rm_y, am2, rm_z, 0)
    d_y = scatter_y(d_c, rd, rd_c, ad1, rd_y, 1)
    d_z = scatter_z(d_y, ad1, rd_y, ad2, rd_z, 1)

    arrive(m_z)
    value = added(am2[z], rm_z, nz - 1)
    mixed[:, :half] = value[:rows].astype(BF16)
    mixed[:, half:] = value[rows:].astype(BF16)
    arrive(d_z)
    value = added(ad2[z], rd_z, nz - 1)
    tgrad[:, :half] = value[:rows, :half].astype(BF16)
    tgrad[:, half:] = value[rows:, :half].astype(BF16)
    kept = value[:rows, half:].astype(BF16).astype(F32)
    rgrad[...] = dot_nt((spot == which_k).astype(F32), kept).astype(BF16)

    for copy in sends:
        copy.wait_send()
    a_drain()
    b_drain()


def weight_grads(
    xs, us, hidden, gate_delta, up_delta, mixed_in, tgrad_in, rgrad_in,
    gg, ug, dg, mixed, tgrad, rgrad,
):
    x = xs[0]
    gg[...] = dot_tn(x, gate_delta[...]).astype(BF16)
    ug[...] = dot_tn(x, up_delta[...]).astype(BF16)
    dg[...] = dot_tn(hidden[...], us[0]).astype(BF16)

    @pl.when(pl.program_id(0) == 0)
    def _():
        mixed[...] = mixed_in[...]
        tgrad[...] = tgrad_in[...]
        rgrad[...] = rgrad_in[...]


def local(shape, tokens, cotangent, router_weight, expert_ids, w_gate, w_up, w_down):
    nz, ny, nc, nr, cap, chunks = shape
    n = nz * ny * nc
    total = n * cap
    rows, top = expert_ids.shape
    width = tokens.shape[1]
    half = width // 2
    ff = w_gate.shape[2]
    tall = 2 * rows
    wide = half + META
    per = n // chunks * tall
    slots = 2 * nz * (1 + (ny - 1) + ny * (nc - 1))
    wide_d = max(ny, nc) - 1
    vmem = pl.BlockSpec(memory_space=pltpu.VMEM)
    anywhere = pl.BlockSpec(memory_space=pl.ANY)
    v = pltpu.VMEM

    def scatter_buffers(w):
        return [
            v((nz, ny, nc, tall, w), BF16),
            v((nc - 1, nz, ny, tall, w), BF16),
            v((nz, ny, tall, w), BF16),
            v((ny - 1, nz, tall, w), BF16),
            v((nz, tall, w), BF16),
            v((nz - 1, tall, w), BF16),
        ]

    dma = pltpu.SemaphoreType.DMA
    flops = 2 * 9 * total * width * ff
    sds = jax.ShapeDtypeStruct
    scratch = [
        v((width, ff), BF16), v((width, ff), BF16), v((ff, width), BF16),
        v((nz, ny, nc, tall, wide), BF16),
        v((nz, ny, nc, tall, half), BF16),
        v((chunks, per, 2 * total), BF16),
        v((nr, 3, total, ff), BF16),
        *scatter_buffers(half),
        *scatter_buffers(wide),
    ]
    held = sum(2 * math.prod(ref.shape) for ref in scratch)
    mixed, tgrad, rgrad, xs, us, hidden, gate_delta, up_delta = pl.pallas_call(
        functools.partial(kernel, shape),
        out_shape=(
            sds((rows, width), BF16),
            sds((rows, width), BF16),
            sds((top, rows), BF16),
            sds((2, total, half), BF16),
            sds((2, total, half), BF16),
            sds((total, ff), BF16),
            sds((total, ff), BF16),
            sds((total, ff), BF16),
        ),
        in_specs=[vmem] * 4 + [anywhere] * 3,
        out_specs=(vmem,) * 8,
        scratch_shapes=[
            *scratch,
            dma((3,)),
            dma((2, slots)), dma((2, slots)),
            dma((3, nr - 1)), dma((3, nr - 1)),
            dma((2, 3, nz, wide_d)), dma((2, 3, nz, wide_d)),
        ],
        compiler_params=pltpu.CompilerParams(
            collective_id=0, has_side_effects=True,
            vmem_limit_bytes=min(60 << 20, 3 * held)),
        cost_estimate=pl.CostEstimate(
            flops=flops, bytes_accessed=6 * width * ff, transcendentals=total * ff),
    )(tokens, cotangent, router_weight.T, expert_ids.T, w_gate[0], w_up[0], w_down[0])

    step = min(half, 256)
    blocks = half // step

    def fixed(*extent):
        return pl.BlockSpec(extent, lambda i: (0,) * len(extent))

    columns = pl.BlockSpec((1, total, step), lambda i: (i // blocks, 0, i % blocks))
    down = pl.BlockSpec((step, ff), lambda i: (i, 0))
    across = pl.BlockSpec((ff, step), lambda i: (0, i))
    small = [fixed(rows, width), fixed(rows, width), fixed(top, rows)]
    gg, ug, dg, mixed, tgrad, rgrad = pl.pallas_call(
        weight_grads,
        grid=(2 * blocks,),
        out_shape=(
            sds((width, ff), BF16), sds((width, ff), BF16), sds((ff, width), BF16),
            sds((rows, width), BF16), sds((rows, width), BF16), sds((top, rows), BF16),
        ),
        in_specs=[columns, columns] + [fixed(total, ff)] * 3 + small,
        out_specs=(down, down, across, *small),
        compiler_params=pltpu.CompilerParams(vmem_limit_bytes=24 << 20),
    )(xs, us, hidden, gate_delta, up_delta, mixed, tgrad, rgrad)
    return (mixed, tgrad, rgrad.T, gg[None], ug[None], dg[None])


def solution(mesh):
    n = mesh.shape["exp"]
    nr = mesh.shape["rep"]

    def step(tokens, cotangent, router_weight, expert_ids, w_gate, w_up, w_down):
        rows, top = expert_ids.shape
        cap = min(rows, max(2, rows * top * 3 // (2 * n)))
        nz, ny, nc = factors(n)
        chunks = max(1, n * 2 * rows // 768)
        while nz % chunks:
            chunks -= 1
        return local(
            (nz, ny, nc, nr, cap, chunks),
            tokens, cotangent, router_weight, expert_ids, w_gate, w_up, w_down)

    return jax.shard_map(
        step,
        mesh=mesh,
        in_specs=(
            P("exp", "rep"),
            P("exp", "rep"),
            P("exp", None),
            P("exp", None),
            P("exp", "rep", None),
            P("exp", "rep", None),
            P("exp", None, "rep"),
        ),
        out_specs=(
            P("exp", "rep"),
            P("exp", "rep"),
            P("exp", None),
            P("exp", "rep", None),
            P("exp", "rep", None),
            P("exp", None, "rep"),
        ),
        check_vma=False,
    )
```

```python
import functools
import math

import jax
import jax.numpy as jnp
from jax import lax
from jax.experimental import pallas as pl
from jax.experimental.pallas import tpu as pltpu
from jax.sharding import PartitionSpec as P

MESH = pl.DeviceIdType.MESH
F32 = jnp.float32
BF16 = jnp.bfloat16
META = 128
SLOT_LANE, WEIGHT_LANE, HALF_LANE = 16, 32, 48


def factors(n):
    nc = 2
    chips = n // nc
    ny = 1 << (int(math.log2(chips)) // 2)
    return chips // ny, ny, nc


def dot(a, b):
    return lax.dot_general(a, b, (((1,), (0,)), ((), ())), preferred_element_type=F32)


def dot_tn(a, b):
    return lax.dot_general(a, b, (((0,), (0,)), ((), ())), preferred_element_type=F32)


def dot_nt(a, b):
    return lax.dot_general(a, b, (((1,), (1,)), ((), ())), preferred_element_type=F32)


def kernel(
    shape, tok, cot, rw, ids, wg_hbm, wu_hbm, wd_hbm,
    mixed, tgrad, rgrad, xs, us, hid_out, gd_out, ud_out,
    wg, wu, wd, mbuf, abuf, bbuf, st, xb,
    rm, rm_c, am1, rm_y, am2, rm_z,
    rd, rd_c, ad1, rd_y, ad2, rd_z,
    wsem, ag_send, ag_recv, x_send, x_recv, rs_send, rs_recv,
):
    nz, ny, nc, nr, cap, chunks = shape
    n = nz * ny * nc
    total = n * cap
    top, rows = ids.shape
    width = tok.shape[1]
    half = width // 2

    me_r = lax.axis_index("rep")
    me = lax.axis_index("exp")
    z = me // (ny * nc)
    y = (me // nc) % ny
    c = me % nc

    def exp_at(zz, yy, cc):
        return (me_r, (zz * ny + yy) * nc + cc)

    z_peers = [exp_at((z + d) % nz, y, c) for d in range(1, nz)]
    y_peers = [exp_at(z, (y + d) % ny, c) for d in range(1, ny)]
    c_peers = [exp_at(z, y, (c + d) % nc) for d in range(1, nc)]
    r_peers = [((me_r + d) % nr, me) for d in range(1, nr)]
    everyone = z_peers + y_peers + c_peers + r_peers

    barrier = pltpu.get_barrier_semaphore()
    for peer in everyone:
        pl.semaphore_signal(barrier, inc=1, device_id=peer, device_id_type=MESH)

    loads = [
        pltpu.make_async_copy(src, dst, wsem.at[i])
        for i, (src, dst) in enumerate(((wg_hbm, wg), (wu_hbm, wu), (wd_hbm, wd)))
    ]
    for load in loads:
        load.start()

    lane = lax.broadcasted_iota(jnp.int32, (rows, META), 1)
    spot = lax.broadcasted_iota(jnp.int32, (top, META), 1)
    which_k = lax.broadcasted_iota(jnp.int32, (top, META), 0)

    def columns(value, at):
        return dot_tn(value.astype(F32), (spot == which_k + at).astype(F32))

    own_ids = columns(ids[...], 0)
    lane_f = lane.astype(F32)
    named = jnp.zeros((rows, META), F32)
    for k in range(top):
        named += (own_ids[:, k:k + 1] == lane_f).astype(F32)
    before = (
        lax.broadcasted_iota(jnp.int32, (rows, rows), 1)
        < lax.broadcasted_iota(jnp.int32, (rows, rows), 0)
    ).astype(F32)
    earlier = dot(before, named)
    meta = own_ids + columns(rw[...], WEIGHT_LANE)
    first_slot = (me * cap).astype(F32)
    for k in range(top):
        id_k = own_ids[:, k:k + 1]
        rank = jnp.sum(jnp.where(id_k == lane_f, earlier, 0.0), axis=1, keepdims=True)
        meta = jnp.where(lane == SLOT_LANE + k, rank + first_slot, meta)
    tok_v = tok[...].astype(F32)
    cot_v = cot[...].astype(F32)
    abuf[z, y, c] = jnp.concatenate(
        [tok_v[:, :half], tok_v[:, half:]], axis=0).astype(BF16)
    mbuf[z, y, c] = jnp.concatenate(
        [meta, jnp.where(lane == HALF_LANE, 1.0, meta)], axis=0).astype(BF16)
    bbuf[z, y, c] = jnp.concatenate(
        [cot_v[:, :half], cot_v[:, half:]], axis=0).astype(BF16)

    pl.semaphore_wait(barrier, len(everyone))

    sends = []

    def send(src, dst, s_sem, r_sem, peer):
        copy = pltpu.make_async_remote_copy(
            src_ref=src, dst_ref=dst, send_sem=s_sem, recv_sem=r_sem,
            device_id=peer, device_id_type=MESH)
        copy.start()
        sends.append(copy)
        return copy

    def arrive(copies):
        for copy in copies:
            copy.wait_recv()

    def gather(buf, which):
        def move(zz, yy, slot, peer):
            block = buf.at[zz, yy, c] if yy is not None else buf.at[zz, y, c]
            return pltpu.make_async_remote_copy(
                src_ref=block, dst_ref=block, send_sem=ag_send.at[which, slot],
                recv_sem=ag_recv.at[which, slot], device_id=peer, device_id_type=MESH)

        up_to = exp_at(jnp.minimum(z + 1, nz - 1), y, c)
        down_to = exp_at(jnp.maximum(z - 1, 0), y, c)
        base_y = 2 * nz
        base_c = base_y + 2 * nz * (ny - 1)

        def over_y(zz, tag):
            return [
                move(zz, y, base_y + tag * (ny - 1) + e, peer)
                for e, peer in enumerate(y_peers)
            ]

        def over_c(zz, tag, some):
            found = []
            for e in some:
                for f, peer in enumerate(c_peers):
                    slot = base_c + (tag * ny + e) * (nc - 1) + f
                    found.append(move(zz, (y + ny - e) % ny, slot, peer))
            return found

        steps = []
        for s in range(nz):
            if s == 0:
                steps.append((0, z, None))
            else:
                steps.append((s, jnp.maximum(z - s, 0), z >= s))
                steps.append((nz + s, jnp.minimum(z + s, nz - 1), z + s < nz))

        def guarded(cond, body):
            if cond is None:
                body()
            else:
                pl.when(cond)(body)

        def links(tag, zz, cond, act):
            own = tag == 0
            if own or tag < nz:
                s = tag
                if s + 1 < nz:
                    more = z + 1 < nz if own else (z >= s) & (z + 1 < nz)
                    guarded(more, lambda: act(move(zz, y, s + 1, up_to)))
            if own or tag > nz:
                s = 0 if own else tag - nz
                if s + 1 < nz:
                    more = z >= 1 if own else (z + s < nz) & (z >= 1)
                    guarded(more, lambda: act(move(zz, y, nz + s + 1, down_to)))

        def begin(tag, zz, cond):
            def body():
                if tag != 0:
                    move(zz, y, tag, up_to).wait_recv()

            guarded(cond, body)
            links(tag, zz, cond, lambda copy: copy.start())

            def rest():
                for copy in over_y(zz, tag):
                    copy.start()
                for copy in over_c(zz, tag, [0]):
                    copy.start()

            guarded(cond, rest)

        def pass_on(tag, zz, cond):
            def body():
                for e, copy in enumerate(over_y(zz, tag)):
                    copy.wait_recv()
                    for onward in over_c(zz, tag, [e + 1]):
                        onward.start()

            guarded(cond, body)

        def finish(tag, zz, cond):
            def body():
                for copy in over_c(zz, tag, range(ny)):
                    copy.wait_recv()

            guarded(cond, body)

        def drain():
            for tag, zz, cond in steps:
                links(tag, zz, cond, lambda copy: copy.wait_send())

                def body(zz=zz, tag=tag):
                    for copy in over_y(zz, tag) + over_c(zz, tag, range(ny)):
                        copy.wait_send()

                guarded(cond, body)

        def first():
            begin(*steps[0])

        def middle(part, parts):
            count = len(steps) - 1
            for i in range(part * count // parts, (part + 1) * count // parts):
                begin(*steps[i + 1])
                pass_on(*steps[i])

        def last():
            pass_on(*steps[-1])
            for step in steps:
                finish(*step)

        return first, middle, last, drain

    a_first, a_middle, a_last, a_drain = gather(abuf, 0)
    b_first, b_middle, b_last, b_drain = gather(bbuf, 1)
    m_first, m_middle, m_last, m_drain = gather(mbuf, 2)
    m_first()
    a_first()
    m_middle(0, 3)
    m_middle(1, 3)
    a_middle(0, 3)
    m_middle(2, 3)
    a_middle(1, 3)
    m_last()

    zs = nz // chunks
    per = zs * ny * nc * 2 * rows

    sc = total // chunks

    def build(i):
        info = mbuf[i * zs:(i + 1) * zs].reshape(per, META).astype(F32)
        lanes = lax.broadcasted_iota(jnp.int32, (per, META), 1)
        match = (info == me.astype(F32)) & (lanes < top)
        slot = jnp.sum(
            jnp.where(match, pltpu.roll(info, META - SLOT_LANE, 1), 0.0)
            + jnp.where(lanes == HALF_LANE, info * sc, 0.0),
            axis=1, keepdims=True)
        found = jnp.sum(match.astype(F32), axis=1, keepdims=True)
        slot = jnp.where(found > 0.0, slot - i * sc, -1.0).astype(jnp.int32)
        place = lax.broadcasted_iota(jnp.int32, (per, 2 * sc), 1) == slot
        st[i] = jnp.where(place, 1.0, 0.0).astype(BF16)

    def gathered(buf, wide):
        found = [
            dot_tn(st[i], buf[i * zs:(i + 1) * zs].reshape(per, wide)) for i in range(chunks)
        ]
        return (jnp.concatenate([part[:sc] for part in found], axis=0),
                jnp.concatenate([part[sc:] for part in found], axis=0))

    def spread(buf, left, right, wide):
        for i in range(chunks):
            rows_i = slice(i * sc, (i + 1) * sc)
            part = jnp.concatenate([left[rows_i], right[rows_i]], axis=0).astype(BF16)
            buf[i * zs:(i + 1) * zs, :, :, :, :wide] = dot(st[i], part).astype(BF16).reshape(
                zs, ny, nc, 2 * rows, wide)

    first_part = max(1, chunks // 2)
    for i in range(first_part):
        build(i)
    a_middle(2, 3)
    b_first()
    for i in range(first_part, chunks):
        build(i)
    info, _ = gathered(mbuf, META)
    lanes = lax.broadcasted_iota(jnp.int32, (total, META), 1)
    match = (info == me.astype(F32)) & (lanes < top)
    slot_w = jnp.sum(
        jnp.where(match, pltpu.roll(info, META - WEIGHT_LANE, 1), 0.0), axis=1, keepdims=True)
    a_last()
    x_left, x_right = gathered(abuf, half)
    xs[0] = x_left.astype(BF16)
    xs[1] = x_right.astype(BF16)
    b_middle(0, 3)

    def exchange(i, value):
        xb[me_r, i] = value.astype(BF16)
        return [
            send(xb.at[me_r, i], xb.at[me_r, i], x_send.at[i, d], x_recv.at[i, d], peer)
            for d, peer in enumerate(r_peers)
        ]

    def summed(i):
        value = xb[0, i].astype(F32)
        for r in range(1, nr):
            value = value + xb[r, i].astype(F32)
        return value

    loads[0].wait()
    x_gate = exchange(0, dot(xs[0], wg[:half]) + dot(xs[1], wg[half:]))
    b_middle(1, 3)
    loads[1].wait()
    x_up = exchange(1, dot(xs[0], wu[:half]) + dot(xs[1], wu[half:]))

    b_middle(2, 3)
    b_last()

    up_left, up_right = gathered(bbuf, half)
    up_left = up_left.astype(BF16)
    up_right = up_right.astype(BF16)
    loads[2].wait()
    x_hid = exchange(2, dot_nt(up_left, wd[:, :half]) + dot_nt(up_right, wd[:, half:]))
    us[0] = (slot_w * up_left.astype(F32)).astype(BF16)
    us[1] = (slot_w * up_right.astype(F32)).astype(BF16)

    def dest(j):
        return (z + j + 1) % nz

    def scatter_core(buf, got, which):
        return [
            [
                send(buf.at[dest(j), :, (c + d + 1) % nc], got.at[d, dest(j)],
                     rs_send.at[which, 0, j, d], rs_recv.at[which, 0, j, d], peer)
                for d, peer in enumerate(c_peers)
            ]
            for j in range(nz)
        ]

    def scatter_y(copies, buf, got, summed_c, got_y, which):
        on = []
        for j in range(nz):
            arrive(copies[j])
            zz = dest(j)
            value = buf[zz, :, c].astype(F32)
            for d in range(nc - 1):
                value = value + got[d, zz].astype(F32)
            summed_c[zz] = value.astype(BF16)
            on.append([
                send(summed_c.at[zz, (y + d + 1) % ny], got_y.at[d, zz],
                     rs_send.at[which, 1, j, d], rs_recv.at[which, 1, j, d], peer)
                for d, peer in enumerate(y_peers)
            ])
        return on

    def scatter_z(copies, summed_c, got_y, summed_y, got_z, which):
        on = []
        for j in range(nz):
            arrive(copies[j])
            zz = dest(j)
            value = summed_c[zz, y].astype(F32)
            for d in range(ny - 1):
                value = value + got_y[d, zz].astype(F32)
            summed_y[zz] = value.astype(BF16)
            if j < nz - 1:
                on.append(
                    send(summed_y.at[zz], got_z.at[j], rs_send.at[which, 2, j, 0],
                         rs_recv.at[which, 2, j, 0], z_peers[j]))
        return on

    def added(own, got, count):
        value = own.astype(F32)
        for d in range(count):
            value = value + got[d].astype(F32)
        return value

    arrive(x_gate)
    arrive(x_up)
    gate = summed(0)
    up = summed(1)
    sig = 1.0 / (1.0 + jnp.exp(-gate))
    active = gate * sig
    hidden32 = active * up
    hidden = hidden32.astype(BF16)

    def weighted(value):
        return slot_w * value.astype(BF16).astype(F32)

    spread(rm, weighted(dot(hidden, wd[:, :half])), weighted(dot(hidden, wd[:, half:])), half)
    m_c = scatter_core(rm, rm_c, 0)
    hid_out[...] = hidden
    m_y = scatter_y(m_c, rm, rm_c, am1, rm_y, 0)

    arrive(x_hid)
    hid_plain = summed(2)
    router = jnp.sum(hidden.astype(F32) * hid_plain, axis=1, keepdims=True)
    hid = slot_w * hid_plain
    gate_delta = (hid * up * sig * (1.0 + gate * (1.0 - sig))).astype(BF16)
    up_delta = (hid * active).astype(BF16)
    spread(
        rd,
        dot_nt(gate_delta, wg[:half]) + dot_nt(up_delta, wu[:half]),
        dot_nt(gate_delta, wg[half:]) + dot_nt(up_delta, wu[half:]),
        half)
    wide_router = jnp.broadcast_to(router, (total, META))
    for i in range(chunks):
        part = wide_router[i * sc:(i + 1) * sc]
        part = jnp.concatenate([part, jnp.zeros((sc, META), F32)], axis=0).astype(BF16)
        info_i = mbuf[i * zs:(i + 1) * zs].reshape(per, META).astype(F32)
        lanes_i = lax.broadcasted_iota(jnp.int32, (per, META), 1)
        hit = (info_i == me.astype(F32)) & (lanes_i < top)
        rd[i * zs:(i + 1) * zs, :, :, :, half:] = jnp.where(
            hit, dot(st[i], part), 0.0).astype(BF16).reshape(zs, ny, nc, 2 * rows, META)
    d_c = scatter_core(rd, rd_c, 1)

    gd_out[...] = gate_delta
    ud_out[...] = up_delta
    m_z = scatter_z(m_y, am1, rm_y, am2, rm_z, 0)
    d_y = scatter_y(d_c, rd, rd_c, ad1, rd_y, 1)
    d_z = scatter_z(d_y, ad1, rd_y, ad2, rd_z, 1)

    arrive(m_z)
    value = added(am2[z], rm_z, nz - 1)
    mixed[:, :half] = value[:rows].astype(BF16)
    mixed[:, half:] = value[rows:].astype(BF16)
    arrive(d_z)
    value = added(ad2[z], rd_z, nz - 1)
    tgrad[:, :half] = value[:rows, :half].astype(BF16)
    tgrad[:, half:] = value[rows:, :half].astype(BF16)
    kept = value[:rows, half:].astype(BF16).astype(F32)
    rgrad[...] = dot_nt((spot == which_k).astype(F32), kept).astype(BF16)

    for copy in sends:
        copy.wait_send()
    a_drain()
    b_drain()
    m_drain()


def weight_grads(
    xs, us, hidden, gate_delta, up_delta, mixed_in, tgrad_in, rgrad_in,
    gg, ug, dg, mixed, tgrad, rgrad,
):
    x = xs[0]
    gg[...] = dot_tn(x, gate_delta[...]).astype(BF16)
    ug[...] = dot_tn(x, up_delta[...]).astype(BF16)
    dg[...] = dot_tn(hidden[...], us[0]).astype(BF16)

    @pl.when(pl.program_id(0) == 0)
    def _():
        mixed[...] = mixed_in[...]
        tgrad[...] = tgrad_in[...]
        rgrad[...] = rgrad_in[...]


def local(shape, tokens, cotangent, router_weight, expert_ids, w_gate, w_up, w_down):
    nz, ny, nc, nr, cap, chunks = shape
    n = nz * ny * nc
    total = n * cap
    rows, top = expert_ids.shape
    width = tokens.shape[1]
    half = width // 2
    ff = w_gate.shape[2]
    tall = 2 * rows
    wide = half + META
    per = n // chunks * tall
    slots = 2 * nz * (1 + (ny - 1) + ny * (nc - 1))
    wide_d = max(ny, nc) - 1
    vmem = pl.BlockSpec(memory_space=pltpu.VMEM)
    anywhere = pl.BlockSpec(memory_space=pl.ANY)
    v = pltpu.VMEM

    def scatter_buffers(w):
        return [
            v((nz, ny, nc, tall, w), BF16),
            v((nc - 1, nz, ny, tall, w), BF16),
            v((nz, ny, tall, w), BF16),
            v((ny - 1, nz, tall, w), BF16),
            v((nz, tall, w), BF16),
            v((nz - 1, tall, w), BF16),
        ]

    dma = pltpu.SemaphoreType.DMA
    flops = 2 * 9 * total * width * ff
    sds = jax.ShapeDtypeStruct
    scratch = [
        v((width, ff), BF16), v((width, ff), BF16), v((ff, width), BF16),
        v((nz, ny, nc, tall, META), BF16),
        v((nz, ny, nc, tall, half), BF16),
        v((nz, ny, nc, tall, half), BF16),
        v((chunks, per, 2 * total // chunks), BF16),
        v((nr, 3, total, ff), BF16),
        *scatter_buffers(half),
        *scatter_buffers(wide),
    ]
    mixed, tgrad, rgrad, xs, us, hidden, gate_delta, up_delta = pl.pallas_call(
        functools.partial(kernel, shape),
        out_shape=(
            sds((rows, width), BF16),
            sds((rows, width), BF16),
            sds((top, rows), BF16),
            sds((2, total, half), BF16),
            sds((2, total, half), BF16),
            sds((total, ff), BF16),
            sds((total, ff), BF16),
            sds((total, ff), BF16),
        ),
        in_specs=[vmem] * 4 + [anywhere] * 3,
        out_specs=(vmem,) * 8,
        scratch_shapes=[
            *scratch,
            dma((3,)),
            dma((3, slots)), dma((3, slots)),
            dma((3, nr - 1)), dma((3, nr - 1)),
            dma((2, 3, nz, wide_d)), dma((2, 3, nz, wide_d)),
        ],
        compiler_params=pltpu.CompilerParams(
            collective_id=0, has_side_effects=True,
            vmem_limit_bytes=60 << 20),
        cost_estimate=pl.CostEstimate(
            flops=flops, bytes_accessed=6 * width * ff, transcendentals=total * ff),
    )(tokens, cotangent, router_weight.T, expert_ids.T, w_gate[0], w_up[0], w_down[0])

    step = min(half, 256)
    blocks = half // step

    def fixed(*extent):
        return pl.BlockSpec(extent, lambda i: (0,) * len(extent))

    columns = pl.BlockSpec((1, total, step), lambda i: (i // blocks, 0, i % blocks))
    down = pl.BlockSpec((step, ff), lambda i: (i, 0))
    across = pl.BlockSpec((ff, step), lambda i: (0, i))
    small = [fixed(rows, width), fixed(rows, width), fixed(top, rows)]
    gg, ug, dg, mixed, tgrad, rgrad = pl.pallas_call(
        weight_grads,
        grid=(2 * blocks,),
        out_shape=(
            sds((width, ff), BF16), sds((width, ff), BF16), sds((ff, width), BF16),
            sds((rows, width), BF16), sds((rows, width), BF16), sds((top, rows), BF16),
        ),
        in_specs=[columns, columns] + [fixed(total, ff)] * 3 + small,
        out_specs=(down, down, across, *small),
        compiler_params=pltpu.CompilerParams(vmem_limit_bytes=60 << 20),
    )(xs, us, hidden, gate_delta, up_delta, mixed, tgrad, rgrad)
    return (mixed, tgrad, rgrad.T, gg[None], ug[None], dg[None])


def solution(mesh):
    n = mesh.shape["exp"]
    nr = mesh.shape["rep"]

    def step(tokens, cotangent, router_weight, expert_ids, w_gate, w_up, w_down):
        rows, top = expert_ids.shape
        cap = min(rows, max(2, rows * top * 3 // (2 * n)))
        nz, ny, nc = factors(n)
        chunks = nz
        while nz % chunks or n * cap // chunks % 8:
            chunks -= 1
        return local(
            (nz, ny, nc, nr, cap, chunks),
            tokens, cotangent, router_weight, expert_ids, w_gate, w_up, w_down)

    return jax.shard_map(
        step,
        mesh=mesh,
        in_specs=(
            P("exp", "rep"),
            P("exp", "rep"),
            P("exp", None),
            P("exp", None),
            P("exp", "rep", None),
            P("exp", "rep", None),
            P("exp", None, "rep"),
        ),
        out_specs=(
            P("exp", "rep"),
            P("exp", "rep"),
            P("exp", None),
            P("exp", "rep", None),
            P("exp", "rep", None),
            P("exp", None, "rep"),
        ),
        check_vma=False,
    )
```

```python
import functools
import math

import jax
import jax.numpy as jnp
from jax import lax
from jax.experimental import pallas as pl
from jax.experimental.pallas import tpu as pltpu
from jax.sharding import PartitionSpec as P

MESH = pl.DeviceIdType.MESH
F32 = jnp.float32
BF16 = jnp.bfloat16
META = 128
SLOT_LANE, WEIGHT_LANE, HALF_LANE = 16, 32, 48


def factors(n):
    nc = 2
    chips = n // nc
    ny = 1 << (int(math.log2(chips)) // 2)
    return chips // ny, ny, nc


def dot(a, b):
    return lax.dot_general(a, b, (((1,), (0,)), ((), ())), preferred_element_type=F32)


def dot_tn(a, b):
    return lax.dot_general(a, b, (((0,), (0,)), ((), ())), preferred_element_type=F32)


def dot_nt(a, b):
    return lax.dot_general(a, b, (((1,), (1,)), ((), ())), preferred_element_type=F32)


def kernel(
    shape, tok_hbm, cot_hbm, rw_hbm, ids_hbm, wg_hbm, wu_hbm, wd_hbm,
    mixed, tgrad, rgrad, xs, us, hid_out, gd_out, ud_out,
    tok, cot, rw, ids, wg, wu, wd, mbuf, abuf, bbuf, st, xb,
    rm, rm_c, am1, rm_y, am2, rm_z,
    rd, rd_c, ad1, rd_y, ad2, rd_z,
    wsem, ag_send, ag_recv, x_send, x_recv, rs_send, rs_recv,
):
    nz, ny, nc, nr, cap, chunks = shape
    n = nz * ny * nc
    total = n * cap
    top, rows = ids.shape
    width = tok.shape[1]
    half = width // 2

    me_r = lax.axis_index("rep")
    me = lax.axis_index("exp")
    z = me // (ny * nc)
    y = (me // nc) % ny
    c = me % nc

    def exp_at(zz, yy, cc):
        return (me_r, (zz * ny + yy) * nc + cc)

    z_peers = [exp_at((z + d) % nz, y, c) for d in range(1, nz)]
    y_peers = [exp_at(z, (y + d) % ny, c) for d in range(1, ny)]
    c_peers = [exp_at(z, y, (c + d) % nc) for d in range(1, nc)]
    r_peers = [((me_r + d) % nr, me) for d in range(1, nr)]
    everyone = z_peers + y_peers + c_peers + r_peers

    inputs = [
        pltpu.make_async_copy(src, dst, wsem.at[3 + i])
        for i, (src, dst) in enumerate(
            ((ids_hbm, ids), (rw_hbm, rw), (tok_hbm, tok), (cot_hbm, cot)))
    ]
    for load in inputs:
        load.start()
    barrier = pltpu.get_barrier_semaphore()
    for peer in everyone:
        pl.semaphore_signal(barrier, inc=1, device_id=peer, device_id_type=MESH)

    loads = [
        pltpu.make_async_copy(src, dst, wsem.at[i])
        for i, (src, dst) in enumerate(((wg_hbm, wg), (wu_hbm, wu), (wd_hbm, wd)))
    ]
    for load in loads:
        load.start()

    for load in inputs:
        load.wait()

    lane = lax.broadcasted_iota(jnp.int32, (rows, META), 1)
    spot = lax.broadcasted_iota(jnp.int32, (top, META), 1)
    which_k = lax.broadcasted_iota(jnp.int32, (top, META), 0)

    def columns(value, at):
        return dot_tn(value.astype(F32), (spot == which_k + at).astype(F32))

    own_ids = columns(ids[...], 0)
    lane_f = lane.astype(F32)
    named = jnp.zeros((rows, META), F32)
    for k in range(top):
        named += (own_ids[:, k:k + 1] == lane_f).astype(F32)
    before = (
        lax.broadcasted_iota(jnp.int32, (rows, rows), 1)
        < lax.broadcasted_iota(jnp.int32, (rows, rows), 0)
    ).astype(F32)
    earlier = dot(before, named)
    meta = own_ids + columns(rw[...], WEIGHT_LANE)
    first_slot = (me * cap).astype(F32)
    for k in range(top):
        id_k = own_ids[:, k:k + 1]
        rank = jnp.sum(jnp.where(id_k == lane_f, earlier, 0.0), axis=1, keepdims=True)
        meta = jnp.where(lane == SLOT_LANE + k, rank + first_slot, meta)
    tok_v = tok[...].astype(F32)
    cot_v = cot[...].astype(F32)
    abuf[z, y, c] = jnp.concatenate(
        [tok_v[:, :half], tok_v[:, half:]], axis=0).astype(BF16)
    mbuf[z, y, c] = jnp.concatenate(
        [meta, jnp.where(lane == HALF_LANE, 1.0, meta)], axis=0).astype(BF16)
    bbuf[z, y, c] = jnp.concatenate(
        [cot_v[:, :half], cot_v[:, half:]], axis=0).astype(BF16)

    pl.semaphore_wait(barrier, len(everyone))

    sends = []

    def send(src, dst, s_sem, r_sem, peer):
        copy = pltpu.make_async_remote_copy(
            src_ref=src, dst_ref=dst, send_sem=s_sem, recv_sem=r_sem,
            device_id=peer, device_id_type=MESH)
        copy.start()
        sends.append(copy)
        return copy

    def arrive(copies):
        for copy in copies:
            copy.wait_recv()

    def gather_stage(buf, which, stage, peers, block):
        return [
            send(block(buf), block(buf), ag_send.at[which, stage, d],
                 ag_recv.at[which, stage, d], peer)
            for d, peer in enumerate(peers)
        ]

    def over_z(buf, which):
        return gather_stage(buf, which, 0, z_peers, lambda ref: ref.at[z, y, c])

    def over_y(buf, which):
        return gather_stage(buf, which, 1, y_peers, lambda ref: ref.at[:, y, c])

    def over_c(buf, which):
        return gather_stage(buf, which, 2, c_peers, lambda ref: ref.at[:, :, c])

    m_z = over_z(mbuf, 2)
    a_z = over_z(abuf, 0)
    arrive(m_z)
    m_y = over_y(mbuf, 2)
    arrive(m_y)
    m_c = over_c(mbuf, 2)
    arrive(a_z)
    a_y = over_y(abuf, 0)
    b_z = over_z(bbuf, 1)
    arrive(m_c)

    zs = nz // chunks
    per = zs * ny * nc * 2 * rows

    sc = total // chunks

    def build(i):
        info = mbuf[i * zs:(i + 1) * zs].reshape(per, META).astype(F32)
        lanes = lax.broadcasted_iota(jnp.int32, (per, META), 1)
        match = (info == me.astype(F32)) & (lanes < top)
        slot = jnp.sum(
            jnp.where(match, pltpu.roll(info, META - SLOT_LANE, 1), 0.0)
            + jnp.where(lanes == HALF_LANE, info * sc, 0.0),
            axis=1, keepdims=True)
        found = jnp.sum(match.astype(F32), axis=1, keepdims=True)
        slot = jnp.where(found > 0.0, slot - i * sc, -1.0).astype(jnp.int32)
        place = lax.broadcasted_iota(jnp.int32, (per, 2 * sc), 1) == slot
        st[i] = jnp.where(place, 1.0, 0.0).astype(BF16)

    def gathered(buf, wide):
        found = [
            dot_tn(st[i], buf[i * zs:(i + 1) * zs].reshape(per, wide)) for i in range(chunks)
        ]
        return (jnp.concatenate([part[:sc] for part in found], axis=0),
                jnp.concatenate([part[sc:] for part in found], axis=0))

    def spread(buf, left, right, wide):
        for i in range(chunks):
            rows_i = slice(i * sc, (i + 1) * sc)
            part = jnp.concatenate([left[rows_i], right[rows_i]], axis=0).astype(BF16)
            buf[i * zs:(i + 1) * zs, :, :, :, :wide] = dot(st[i], part).astype(BF16).reshape(
                zs, ny, nc, 2 * rows, wide)

    for i in range(chunks):
        build(i)
    arrive(a_y)
    a_c = over_c(abuf, 0)
    arrive(b_z)
    b_y = over_y(bbuf, 1)
    info, _ = gathered(mbuf, META)
    lanes = lax.broadcasted_iota(jnp.int32, (total, META), 1)
    match = (info == me.astype(F32)) & (lanes < top)
    slot_w = jnp.sum(
        jnp.where(match, pltpu.roll(info, META - WEIGHT_LANE, 1), 0.0), axis=1, keepdims=True)
    arrive(a_c)
    x_left, x_right = gathered(abuf, half)
    xs[0] = x_left.astype(BF16)
    xs[1] = x_right.astype(BF16)
    def exchange(i, value):
        xb[me_r, i] = value.astype(BF16)
        return [
            send(xb.at[me_r, i], xb.at[me_r, i], x_send.at[i, d], x_recv.at[i, d], peer)
            for d, peer in enumerate(r_peers)
        ]

    def summed(i):
        value = xb[0, i].astype(F32)
        for r in range(1, nr):
            value = value + xb[r, i].astype(F32)
        return value

    loads[0].wait()
    x_gate = exchange(0, dot(xs[0], wg[:half]) + dot(xs[1], wg[half:]))
    loads[1].wait()
    x_up = exchange(1, dot(xs[0], wu[:half]) + dot(xs[1], wu[half:]))

    arrive(b_y)
    b_c = over_c(bbuf, 1)
    arrive(b_c)

    up_left, up_right = gathered(bbuf, half)
    up_left = up_left.astype(BF16)
    up_right = up_right.astype(BF16)
    loads[2].wait()
    x_hid = exchange(2, dot_nt(up_left, wd[:, :half]) + dot_nt(up_right, wd[:, half:]))
    us[0] = (slot_w * up_left.astype(F32)).astype(BF16)
    us[1] = (slot_w * up_right.astype(F32)).astype(BF16)

    def scatter(block, got, which, stage, peers):
        return [
            send(block(d + 1), got.at[d], rs_send.at[which, stage, d],
                 rs_recv.at[which, stage, d], peer)
            for d, peer in enumerate(peers)
        ]

    def scatter_core(buf, got, which):
        return scatter(lambda d: buf.at[:, :, (c + d) % nc], got, which, 0, c_peers)

    def scatter_y(copies, buf, got, summed_c, got_y, which):
        arrive(copies)
        summed_c[...] = added(buf[:, :, c], got, nc - 1).astype(BF16)
        return scatter(lambda d: summed_c.at[:, (y + d) % ny], got_y, which, 1, y_peers)

    def scatter_z(copies, summed_c, got_y, summed_y, got_z, which):
        arrive(copies)
        summed_y[...] = added(summed_c[:, y], got_y, ny - 1).astype(BF16)
        return scatter(lambda d: summed_y.at[(z + d) % nz], got_z, which, 2, z_peers)

    def added(own, got, count):
        value = own.astype(F32)
        for d in range(count):
            value = value + got[d].astype(F32)
        return value

    arrive(x_gate)
    arrive(x_up)
    gate = summed(0)
    up = summed(1)
    sig = 1.0 / (1.0 + jnp.exp(-gate))
    active = gate * sig
    hidden32 = active * up
    hidden = hidden32.astype(BF16)

    def weighted(value):
        return slot_w * value.astype(BF16).astype(F32)

    spread(rm, weighted(dot(hidden, wd[:, :half])), weighted(dot(hidden, wd[:, half:])), half)
    m_c = scatter_core(rm, rm_c, 0)
    hid_out[...] = hidden
    m_y = scatter_y(m_c, rm, rm_c, am1, rm_y, 0)

    arrive(x_hid)
    hid_plain = summed(2)
    router = jnp.sum(hidden.astype(F32) * hid_plain, axis=1, keepdims=True)
    hid = slot_w * hid_plain
    gate_delta = (hid * up * sig * (1.0 + gate * (1.0 - sig))).astype(BF16)
    up_delta = (hid * active).astype(BF16)
    spread(
        rd,
        dot_nt(gate_delta, wg[:half]) + dot_nt(up_delta, wu[:half]),
        dot_nt(gate_delta, wg[half:]) + dot_nt(up_delta, wu[half:]),
        half)
    wide_router = jnp.broadcast_to(router, (total, META))
    for i in range(chunks):
        part = wide_router[i * sc:(i + 1) * sc]
        part = jnp.concatenate([part, jnp.zeros((sc, META), F32)], axis=0).astype(BF16)
        info_i = mbuf[i * zs:(i + 1) * zs].reshape(per, META).astype(F32)
        lanes_i = lax.broadcasted_iota(jnp.int32, (per, META), 1)
        hit = (info_i == me.astype(F32)) & (lanes_i < top)
        rd[i * zs:(i + 1) * zs, :, :, :, half:] = jnp.where(
            hit, dot(st[i], part), 0.0).astype(BF16).reshape(zs, ny, nc, 2 * rows, META)
    d_c = scatter_core(rd, rd_c, 1)

    gd_out[...] = gate_delta
    ud_out[...] = up_delta
    m_z = scatter_z(m_y, am1, rm_y, am2, rm_z, 0)
    d_y = scatter_y(d_c, rd, rd_c, ad1, rd_y, 1)
    d_z = scatter_z(d_y, ad1, rd_y, ad2, rd_z, 1)

    arrive(m_z)
    value = added(am2[z], rm_z, nz - 1)
    mixed[:, :half] = value[:rows].astype(BF16)
    mixed[:, half:] = value[rows:].astype(BF16)
    arrive(d_z)
    value = added(ad2[z], rd_z, nz - 1)
    tgrad[:, :half] = value[:rows, :half].astype(BF16)
    tgrad[:, half:] = value[rows:, :half].astype(BF16)
    kept = value[:rows, half:].astype(BF16).astype(F32)
    rgrad[...] = dot_nt((spot == which_k).astype(F32), kept).astype(BF16)

    for copy in sends:
        copy.wait_send()


def weight_grads(
    xs, us, hidden, gate_delta, up_delta, mixed_in, tgrad_in, rgrad_in,
    gg, ug, dg, mixed, tgrad, rgrad,
):
    x = xs[0]
    gg[...] = dot_tn(x, gate_delta[...]).astype(BF16)
    ug[...] = dot_tn(x, up_delta[...]).astype(BF16)
    dg[...] = dot_tn(hidden[...], us[0]).astype(BF16)

    @pl.when(pl.program_id(0) == 0)
    def _():
        mixed[...] = mixed_in[...]
        tgrad[...] = tgrad_in[...]
        rgrad[...] = rgrad_in[...]


def local(shape, tokens, cotangent, router_weight, expert_ids, w_gate, w_up, w_down):
    nz, ny, nc, nr, cap, chunks = shape
    n = nz * ny * nc
    total = n * cap
    rows, top = expert_ids.shape
    width = tokens.shape[1]
    half = width // 2
    ff = w_gate.shape[2]
    tall = 2 * rows
    wide = half + META
    per = n // chunks * tall
    deep = max(nz, ny, nc) - 1
    vmem = pl.BlockSpec(memory_space=pltpu.VMEM)
    anywhere = pl.BlockSpec(memory_space=pl.ANY)
    v = pltpu.VMEM

    def scatter_buffers(w):
        return [
            v((nz, ny, nc, tall, w), BF16),
            v((nc - 1, nz, ny, tall, w), BF16),
            v((nz, ny, tall, w), BF16),
            v((ny - 1, nz, tall, w), BF16),
            v((nz, tall, w), BF16),
            v((nz - 1, tall, w), BF16),
        ]

    dma = pltpu.SemaphoreType.DMA
    flops = 2 * 9 * total * width * ff
    sds = jax.ShapeDtypeStruct
    scratch = [
        v((rows, width), BF16), v((rows, width), BF16),
        v((top, rows), BF16), v((top, rows), jnp.int32),
        v((width, ff), BF16), v((width, ff), BF16), v((ff, width), BF16),
        v((nz, ny, nc, tall, META), BF16),
        v((nz, ny, nc, tall, half), BF16),
        v((nz, ny, nc, tall, half), BF16),
        v((chunks, per, 2 * total // chunks), BF16),
        v((nr, 3, total, ff), BF16),
        *scatter_buffers(half),
        *scatter_buffers(wide),
    ]
    mixed, tgrad, rgrad, xs, us, hidden, gate_delta, up_delta = pl.pallas_call(
        functools.partial(kernel, shape),
        out_shape=(
            sds((rows, width), BF16),
            sds((rows, width), BF16),
            sds((top, rows), BF16),
            sds((2, total, half), BF16),
            sds((2, total, half), BF16),
            sds((total, ff), BF16),
            sds((total, ff), BF16),
            sds((total, ff), BF16),
        ),
        in_specs=[anywhere] * 7,
        out_specs=(vmem,) * 8,
        scratch_shapes=[
            *scratch,
            dma((7,)),
            dma((3, 3, deep)), dma((3, 3, deep)),
            dma((3, nr - 1)), dma((3, nr - 1)),
            dma((2, 3, deep)), dma((2, 3, deep)),
        ],
        compiler_params=pltpu.CompilerParams(
            collective_id=0, has_side_effects=True,
            vmem_limit_bytes=60 << 20),
        cost_estimate=pl.CostEstimate(
            flops=flops, bytes_accessed=6 * width * ff, transcendentals=total * ff),
    )(tokens, cotangent, router_weight.T, expert_ids.T, w_gate[0], w_up[0], w_down[0])

    step = min(half, 256)
    blocks = half // step

    def fixed(*extent):
        return pl.BlockSpec(extent, lambda i: (0,) * len(extent))

    columns = pl.BlockSpec((1, total, step), lambda i: (i // blocks, 0, i % blocks))
    down = pl.BlockSpec((step, ff), lambda i: (i, 0))
    across = pl.BlockSpec((ff, step), lambda i: (0, i))
    small = [fixed(rows, width), fixed(rows, width), fixed(top, rows)]
    gg, ug, dg, mixed, tgrad, rgrad = pl.pallas_call(
        weight_grads,
        grid=(2 * blocks,),
        out_shape=(
            sds((width, ff), BF16), sds((width, ff), BF16), sds((ff, width), BF16),
            sds((rows, width), BF16), sds((rows, width), BF16), sds((top, rows), BF16),
        ),
        in_specs=[columns, columns] + [fixed(total, ff)] * 3 + small,
        out_specs=(down, down, across, *small),
        compiler_params=pltpu.CompilerParams(vmem_limit_bytes=60 << 20),
    )(xs, us, hidden, gate_delta, up_delta, mixed, tgrad, rgrad)
    return (mixed, tgrad, rgrad.T, gg[None], ug[None], dg[None])


def solution(mesh):
    n = mesh.shape["exp"]
    nr = mesh.shape["rep"]

    def step(tokens, cotangent, router_weight, expert_ids, w_gate, w_up, w_down):
        rows, top = expert_ids.shape
        cap = min(rows, max(2, rows * top * 3 // (2 * n)))
        nz, ny, nc = factors(n)
        chunks = nz
        while nz % chunks or n * cap // chunks % 8:
            chunks -= 1
        return local(
            (nz, ny, nc, nr, cap, chunks),
            tokens, cotangent, router_weight, expert_ids, w_gate, w_up, w_down)

    return jax.shard_map(
        step,
        mesh=mesh,
        in_specs=(
            P("exp", "rep"),
            P("exp", "rep"),
            P("exp", None),
            P("exp", None),
            P("exp", "rep", None),
            P("exp", "rep", None),
            P("exp", None, "rep"),
        ),
        out_specs=(
            P("exp", "rep"),
            P("exp", "rep"),
            P("exp", None),
            P("exp", "rep", None),
            P("exp", "rep", None),
            P("exp", None, "rep"),
        ),
        check_vma=False,
    )
```
